32 devices in a mesh: req: 4 (over z), vocab: 8 (over y, x, core).
Axes of the slice: x: 2, y: 2, z: 4, core: 2. Of those that a mesh axis runs over, the one named last changes fastest.
Arguments:
- hidden: bfloat16 [16, 384, 2048], P('req', 'vocab'), may hold values from -80 to 80
- norm_gain: float32 [2048], replicated, may hold values from 0.6 to 1.4
- head_weight: bfloat16 [2048, 32000], P(None, 'vocab'), may hold values from -2 to 2
- token_ids: int32 [16, 384], P('req', 'vocab'), may hold values from 0 to 31999
- lengths: int32 [16], replicated, may hold values from 1 to 384, 3840 in all
- group_ids: int32 [16], replicated, may hold values from 0 to 3
Outputs:
- logprob: float32 [16, 384], P('req', 'vocab')
- entropy: float32 [16, 384], P('req', 'vocab')
- centered: float32 [16], replicated
The draws below stay inside these ranges and needn't reach their ends.
Inputs may be any that keep to these rules, and one draw needn't show every extreme that they name: The lengths sum to 3840; the longest is 384.
All inputs are finite; a program needn't handle non-finite values.
Results may differ from the reference program's by a relative error of at most 0.00093.
Values may be sent and summed in bfloat16 or wider, within the bound.
A program may use at most 128 MiB of HBM per device.

```python
import math
import jax
import jax.numpy as jnp
import numpy as np
from jax import lax

D = 2048
V = 32000
GROUPS = 4
REQS = 16
LEN = 384
LIVE = 3840


def planted_columns(key):
    signs = jnp.where(jax.random.normal(jax.random.fold_in(key, 111), (D, 4), jnp.float32) > 0.0, 1.0, -1.0)
    strength = min(1.9, 160.0 / D) * (0.85 + 0.05 * jnp.arange(4, dtype=jnp.float32))
    first_mag = jax.random.uniform(jax.random.fold_in(key, 112), (D, 4), jnp.float32, 0.9, 1.0)
    second_mag = jax.random.uniform(jax.random.fold_in(key, 113), (D, 4), jnp.float32, 0.9, 1.0)
    even_cols = signs * first_mag * strength[None, :]
    odd_cols = signs * second_mag * strength[None, :] * 0.985
    return (even_cols, odd_cols)


def base_head(key):
    weight = jnp.clip(jax.random.normal(jax.random.fold_in(key, 101), (D, V), jnp.float32), -6.0, 6.0)
    weight = jnp.clip(weight * (3.0 / math.sqrt(D)), -2.0, 2.0)
    even_cols, odd_cols = planted_columns(key)
    planted = jnp.stack([even_cols, odd_cols], axis=2).reshape(D, 8)
    return weight.at[:, 0:8].set(planted)


def draw_head_weight(key, part):
    return base_head(key).astype(jnp.bfloat16)


def draw_hidden(key, part):
    values = jnp.clip(jax.random.normal(jax.random.fold_in(key, 202), (REQS, LEN, D), jnp.float32), -6.0, 6.0)
    even_cols, odd_cols = planted_columns(key)
    aligned = jnp.transpose(even_cols) * 20.0
    values = values.at[:, 0:4, :].set(jnp.broadcast_to(aligned[None, :, :], (REQS, 4, D)))
    return values.astype(jnp.bfloat16)


def with_ends(values, key, smallest, largest):
    shape = values.shape
    spot = [jax.random.randint(jax.random.fold_in(key, axis), (), 0, shape[axis]) for axis in range(len(shape))]
    values = values.at[tuple(spot)].set(smallest)
    longest = shape.index(max(shape))
    spot[longest] = (spot[longest] + 1) % shape[longest]
    return values.at[tuple(spot)].set(largest)


def rank_bounds(count, lean):
    portions = [(1 << 20) // math.isqrt(rank ** lean) + 1 for rank in range(1, count + 1)]
    deviation = 1 + sum(portions) // (1 << 30)
    return np.cumsum(np.array([max(1, weight // deviation) for weight in portions]))


def skewed_ids(own_key, shape, count, slope):
    listing = rank_bounds(count, slope)
    ticket = jax.random.randint(jax.random.fold_in(own_key, 1), shape, 0, int(listing[count - 1]))
    standing = jnp.searchsorted(jnp.asarray(listing, jnp.int32), ticket, side="right")
    return jax.random.permutation(jax.random.fold_in(own_key, 2), count)[standing].astype(jnp.int32)


def length_profile(amount, total, limit, slope):
    loads = [(1 << 20) // math.isqrt(standing ** slope) + 1 for standing in range(2, amount + 1)]
    surplus, holding = total - limit - (amount - 1), [1] * (amount - 1)
    while surplus > 0:
        movable = [i for i in range(amount - 1) if holding[i] < limit]
        whole, budget = sum([loads[i] for i in movable]), surplus
        for i in movable:
            extra = min(limit - holding[i], max(1, budget * loads[i] // whole), surplus)
            holding[i] = holding[i] + extra
            surplus = surplus - extra
    return np.array([limit] + holding)


def ragged(own_key, count, total, bound, skew):
    if count == 2:
        one = jax.random.randint(own_key, (), max(1, total - bound), min(bound, total - 1) + 1)
        return jnp.stack([one, total - one])
    sizes = jnp.asarray(length_profile(count, total, bound, skew), jnp.int32)
    couples = (count - 1) // 2
    donor, taker = sizes[1:1 + 2 * couples:2], sizes[2:2 + 2 * couples:2]
    margin = jnp.minimum(donor - 1, bound - taker)
    moved = jax.random.randint(jax.random.fold_in(own_key, 1), (couples,), 0, 1 << 20) % (margin + 1)
    sizes = sizes.at[1:1 + 2 * couples:2].set(donor - moved).at[2:2 + 2 * couples:2].set(taker + moved)
    return sizes[jax.random.permutation(jax.random.fold_in(own_key, 2), count)]


def setup_inputs(seed: int = 0) -> dict:
    arg_keys = jax.random.split(jax.random.key(seed), 7)
    hidden = draw_hidden(jax.random.fold_in(arg_keys[6], 71), 0)
    norm_gain = jnp.clip(1.0 + 0.08 * jax.random.normal(arg_keys[1], (D,), jnp.float32), 0.6, 1.4)
    head_weight = draw_head_weight(jax.random.fold_in(arg_keys[6], 71), 0)
    token_ids = with_ends(skewed_ids(arg_keys[3], (REQS, LEN), V, 2), jax.random.fold_in(arg_keys[3], 3), 0, V - 1).astype(jnp.int32)
    lengths = ragged(arg_keys[4], REQS, LIVE, LEN, 2).astype(jnp.int32)
    group_ids = with_ends(jax.random.randint(arg_keys[5], (REQS,), 0, GROUPS), jax.random.fold_in(arg_keys[5], 1), 0, GROUPS - 1).astype(jnp.int32)
    return dict(hidden=hidden, norm_gain=norm_gain, head_weight=head_weight, token_ids=token_ids, lengths=lengths, group_ids=group_ids)


norm_eps = 1e-06

def block_stats(block_rows, block_tokens, weight):
    logits = jnp.dot(block_rows, weight, preferred_element_type=jnp.float32)
    row_top = lax.optimization_barrier(jnp.max(logits, axis=1))
    exps = jnp.exp(logits - row_top[:, None])
    exp_total = lax.optimization_barrier(jnp.sum(exps, axis=1))
    moment = lax.optimization_barrier(jnp.sum(exps * logits, axis=1))
    columns = jnp.arange(weight.shape[1], dtype=jnp.int32)
    picked = lax.optimization_barrier(jnp.sum(jnp.where(columns[None, :] == block_tokens[:, None], logits, 0.0), axis=1))
    return (row_top, exp_total, moment, picked)

def reference(hidden, norm_gain, head_weight, token_ids, lengths, group_ids):
    block_len = math.gcd(LEN, 512)

    def one_request(packed):
        rows, tokens = packed
        values = rows.astype(jnp.float32)
        squares = lax.optimization_barrier(jnp.mean(values * values, axis=-1, keepdims=True))
        normed = (values * lax.rsqrt(squares + norm_eps) * norm_gain.astype(jnp.float32)).astype(jnp.bfloat16)

        def one_block(inner):
            return block_stats(inner[0], inner[1], head_weight)
        row_top, exp_total, moment, picked = lax.map(one_block, (normed.reshape(LEN // block_len, block_len, D), tokens.reshape(LEN // block_len, block_len)))
        row_top = row_top.reshape(LEN)
        exp_total = exp_total.reshape(LEN)
        moment = moment.reshape(LEN)
        picked = picked.reshape(LEN)
        log_total = row_top + jnp.log(exp_total)
        return (picked - log_total, log_total - moment / exp_total)
    raw_logprob, raw_entropy = lax.map(one_request, (hidden, token_ids))
    positions = jnp.arange(LEN, dtype=jnp.int32)
    is_live = positions[None, :] < lengths[:, None]
    logprob = jnp.where(is_live, raw_logprob, 0.0)
    entropy = jnp.where(is_live, raw_entropy, 0.0)
    seq_sum = lax.optimization_barrier(jnp.sum(logprob, axis=1))
    same = (group_ids[:, None] == group_ids[None, :]).astype(jnp.float32)
    members = lax.optimization_barrier(jnp.sum(same, axis=1))
    group_mean = lax.optimization_barrier(jnp.sum(same * seq_sum[None, :], axis=1)) / members
    spread = lax.optimization_barrier(jnp.sum(same * (seq_sum[None, :] - group_mean[:, None]) ** 2, axis=1)) / members
    group_std = jnp.maximum(jnp.sqrt(spread), 1.0)
    centered = (seq_sum - group_mean) / group_std
    return (logprob, entropy, centered)
```

```python
import functools
import jax
import jax.numpy as jnp
from jax import lax
from jax.sharding import PartitionSpec as P
from jax.experimental import pallas as pl
from jax.experimental.pallas import tpu as pltpu

norm_eps = 1e-06
BLOCK = 192
MESH_ID = pl.DeviceIdType.MESH
LOW = -1e30
LANES = 128
CHUNK = 512
STRIP = 32
QUARTERS = 4


def piece_order():
    order = [(0, q) for q in range(4)] + [(1, q) for q in range(4)]
    for k in range(4):
        other = (k + 2) % 4
        order += [(2, k), (4, other), (3, k), (5, other)]
    for k in range(2):
        order += [(6, k), (6, k + 2), (7, k), (7, k + 2)]
    return order


def fused_kernel(
    planes, lengths_ref, groups_ref, hidden_ref, gain_ref, tokens_ref, weight_ref,
    logprob_ref, entropy_ref, centered_ref,
    rows, weight, logits_a, logits_b, top_lane, top_row, sum_acc, mom_acc, pick_acc, ids,
    tokens, stat_out, stat_in, part, plane_sums,
    weight_sem, row_send, row_recv, token_send, token_recv, stat_send, stat_recv,
    part_send, part_recv, plane_send, plane_recv,
):
    req_dev, pos_dev, width = hidden_ref.shape
    vocab_dev = weight_ref.shape[1]
    block = ids.shape[0]
    per_block = block // pos_dev
    plane = lax.axis_index("req")
    me = lax.axis_index("vocab")
    order = piece_order()
    slot = {piece: i * pos_dev for i, piece in enumerate(order)}
    blocks = len(order) // per_block
    full = vocab_dev // CHUNK
    tail_start = full * CHUNK

    yy, xx, cc = me // 4, (me // 2) % 2, me % 2

    def partner(rel):
        y = 1 - yy if rel & 4 else yy
        x = 1 - xx if rel & 2 else xx
        c = 1 - cc if rel & 1 else cc
        return (plane, y * 4 + x * 2 + c)

    bounds = list(range(0, tail_start, 2 * CHUNK)) + [vocab_dev]
    if len(bounds) > 2 and bounds[-1] - bounds[-2] < 128:
        bounds.pop(-2)
    spans = list(zip(bounds[:-1], bounds[1:]))
    weight_copies = [
        pltpu.make_async_copy(
            weight_ref.at[:, lo:hi], weight.at[:, lo:hi], weight_sem.at[i]
        )
        for i, (lo, hi) in enumerate(spans)
    ]
    for copy in weight_copies:
        copy.start()

    barrier = pltpu.get_barrier_semaphore()
    for rel in range(1, 8):
        pl.semaphore_signal(barrier, inc=1, device_id=partner(rel), device_id_type=MESH_ID)
    for step in range(1, planes):
        pl.semaphore_signal(
            barrier, inc=1, device_id=(lax.rem(plane + step, planes), me), device_id_type=MESH_ID
        )

    def normalize(q):
        values = hidden_ref[q].astype(jnp.float32)
        squares = jnp.mean(values * values, axis=1, keepdims=True)
        normed = values * lax.rsqrt(squares + norm_eps) * gain_ref[...]
        rows[slot[(0, q)] : slot[(0, q)] + pos_dev, :] = normed.astype(jnp.bfloat16)

    started = []
    send_count = [0]

    def send_piece(piece, rel, landing):
        index = send_count[0]
        send_count[0] += 1
        copy = pltpu.make_async_remote_copy(
            src_ref=rows.at[pl.ds(slot[piece], pos_dev), :],
            dst_ref=rows.at[pl.ds(slot[landing], pos_dev), :],
            send_sem=row_send.at[index],
            recv_sem=row_recv.at[order.index(landing)],
            device_id=partner(rel),
            device_id_type=MESH_ID,
        )
        copy.start()
        started.append(copy)

    def await_piece(piece):
        view = rows.at[pl.ds(slot[piece], pos_dev), :]
        pltpu.make_async_copy(view, view, row_recv.at[order.index(piece)]).wait()

    normalize(0)
    normalize(2)
    tokens[0, :, :] = jnp.zeros(tokens.shape[1:], jnp.int32)
    tokens[0, 0:req_dev, 0:pos_dev] = tokens_ref[...]
    pl.semaphore_wait(barrier, 7 + planes - 1)
    for q_x, q_y in ((0, 2), (1, 3), (2, 0), (3, 1)):
        if q_x == 1:
            normalize(1)
            normalize(3)
        send_piece((0, q_x), 2, (2, q_x))
        send_piece((0, q_y), 4, (4, q_y))
        if q_x == 0:
            for rel in range(1, 8):
                copy = pltpu.make_async_remote_copy(
                    src_ref=tokens.at[0], dst_ref=tokens.at[rel],
                    send_sem=token_send.at[rel], recv_sem=token_recv.at[rel],
                    device_id=partner(rel), device_id_type=MESH_ID,
                )
                copy.start()
                started.append(copy)
        send_piece((0, q_x), 1, (1, q_x))

    def forward(index):
        for rel, q in order[index * 4 : index * 4 + 4]:
            if rel % 2:
                continue
            await_piece((rel, q))
            if rel == 2 and q < 2:
                send_piece((rel, q), 4, (6, q))
            if rel == 4 and q >= 2:
                send_piece((rel, q), 2, (6, q))
            send_piece((rel, q), 1, (rel + 1, q))

    lane_row = lax.broadcasted_iota(jnp.int32, (pos_dev, LANES), 1)
    eye = lane_row == lax.broadcasted_iota(jnp.int32, (pos_dev, LANES), 0)
    logits_a[:, full * CHUNK :] = jnp.full((block, logits_a.shape[1] - full * CHUNK), LOW, jnp.float32)
    logits_b[:, full * CHUNK :] = jnp.full((block, logits_b.shape[1] - full * CHUNK), LOW, jnp.float32)
    for rel in range(8):
        stat_out[rel, :, :] = jnp.zeros(stat_out.shape[1:], jnp.float32)

    def matmul_part(index, out, start, size):
        acc = jnp.dot(
            rows[index * block : (index + 1) * block, :],
            weight[:, pl.ds(start, size)],
            preferred_element_type=jnp.float32,
        )
        out[:, pl.ds(start, size)] = acc
        whole = size // LANES * LANES
        if whole:
            top = acc[:, 0:LANES]
            for j in range(LANES, whole, LANES):
                top = jnp.maximum(top, acc[:, j : j + LANES])
            top_lane[...] = jnp.maximum(top_lane[...], top)
        if whole != size:
            top_lane[...] = jnp.maximum(top_lane[...], out[:, pl.ds(start + whole, LANES)])

    def stats_part(source, start):
        for strip in range(0, block, STRIP):
            r = slice(strip, strip + STRIP)
            total, moment, picked = sum_acc[r, :], mom_acc[r, :], pick_acc[r, :]
            top, local = top_row[r, :], ids[r, :]
            for j in range(0, CHUNK, LANES):
                value = source[r, pl.ds(start + j, LANES)]
                shifted = value - top
                grown = jnp.exp(shifted)
                total = total + grown
                moment = moment + grown * shifted
                picked = jnp.where(local == start + j, value, picked)
            sum_acc[r, :], mom_acc[r, :], pick_acc[r, :] = total, moment, picked

    def begin_stats(index):
        top = jnp.max(top_lane[...], axis=1, keepdims=True)
        top_row[...] = jnp.broadcast_to(top, top_row.shape)
        zero = jnp.zeros((block, LANES), jnp.float32)
        sum_acc[...] = zero
        mom_acc[...] = zero
        pick_acc[...] = zero
        for i in range(per_block):
            rel, q = order[index * per_block + i]
            line = tokens[rel, q : q + 1, :].astype(jnp.float32)
            column = jnp.sum(jnp.where(eye, line, 0.0), axis=1, keepdims=True).astype(jnp.int32)
            local = column - me * vocab_dev
            local = jnp.where(local < vocab_dev, local, -1)
            ids[i * pos_dev : (i + 1) * pos_dev, :] = local - lane_row

    def end_stats(index):
        for i in range(per_block):
            rel, q = order[index * per_block + i]
            r = slice(i * pos_dev, (i + 1) * pos_dev)
            columns = (
                top_row[r, :],
                jnp.sum(sum_acc[r, :], axis=1, keepdims=True),
                jnp.sum(mom_acc[r, :], axis=1, keepdims=True),
                jnp.sum(pick_acc[r, :], axis=1, keepdims=True),
            )
            for s, column in enumerate(columns):
                line = jnp.sum(jnp.where(eye, column, 0.0), axis=0, keepdims=True)
                stat_out[rel, s * 8 + q : s * 8 + q + 1, :] = line
        done = order[: (index + 1) * per_block]
        for rel in range(1, 8):
            last = max(order.index((rel, q)) for q in range(4)) // per_block
            if last == index:
                copy = pltpu.make_async_remote_copy(
                    src_ref=stat_out.at[rel], dst_ref=stat_in.at[rel],
                    send_sem=stat_send.at[rel], recv_sem=stat_recv.at[rel],
                    device_id=partner(rel), device_id_type=MESH_ID,
                )
                copy.start()
                started.append(copy)

    padded = logits_a.shape[1] // CHUNK
    for index in range(blocks + 1):
        current, previous = (logits_a, logits_b) if index % 2 == 0 else (logits_b, logits_a)
        if 1 <= index < blocks:
            ahead = range((index + 1) * per_block // 4, (index + 2) * per_block // 4)
            for part_index in ahead:
                if 2 <= part_index < len(order) // 4:
                    forward(part_index)
            for piece in order[index * per_block : (index + 1) * per_block]:
                if piece[0] % 2:
                    await_piece(piece)
        if index == 1:
            for rel in range(1, 8):
                pltpu.make_async_copy(tokens.at[rel], tokens.at[rel], token_recv.at[rel]).wait()
        if index > 0:
            begin_stats(index - 1)
        if index == blocks:
            @pl.loop(0, padded)
            def drain(n):
                stats_part(previous, pl.multiple_of(n * CHUNK, CHUNK))
        else:
            top_lane[...] = jnp.full((block, LANES), LOW, jnp.float32)
            if index == 0:
                for copy, (lo, hi) in zip(weight_copies, spans):
                    copy.wait()
                    stop = min(hi, tail_start)

                    @pl.loop(lo // CHUNK, stop // CHUNK)
                    def first(n):
                        matmul_part(0, current, pl.multiple_of(n * CHUNK, CHUNK), CHUNK)
            else:
                @pl.loop(0, full)
                def steady(n):
                    start = pl.multiple_of(n * CHUNK, CHUNK)
                    matmul_part(index, current, start, CHUNK)
                    stats_part(previous, start)
            if tail_start < vocab_dev:
                matmul_part(index, current, tail_start, vocab_dev - tail_start)
            if index > 0:
                for n in range(full, padded):
                    stats_part(previous, n * CHUNK)
        if index > 0:
            end_stats(index - 1)

    for rel in range(1, 8):
        pltpu.make_async_copy(stat_in.at[rel], stat_in.at[rel], stat_recv.at[rel]).wait()

    def held(rel, s):
        source = stat_out if rel == 0 else stat_in
        return source[rel, s * 8 : s * 8 + 8, :]

    top = held(0, 0)
    for rel in range(1, 8):
        top = jnp.maximum(top, held(rel, 0))
    total = moment = picked = None
    for rel in range(8):
        gap = held(rel, 0) - top
        scale = jnp.exp(gap)
        one = held(rel, 1) * scale
        two = held(rel, 2) * scale + one * gap
        three = held(rel, 3)
        total = one if total is None else total + one
        moment = two if moment is None else moment + two
        picked = three if picked is None else picked + three
    row_id = lax.broadcasted_iota(jnp.int32, (8, LANES), 0)
    lane_id = lax.broadcasted_iota(jnp.int32, (8, LANES), 1)
    limit = jnp.zeros((8, LANES), jnp.int32)
    for j in range(req_dev):
        limit = jnp.where(row_id == j, lengths_ref[plane * req_dev + j], limit)
    live = (lane_id < pos_dev) & (lane_id + me * pos_dev < limit)
    total = jnp.where(live, total, 1.0)
    log_sum = jnp.log(total)
    logprob = jnp.where(live, picked - top - log_sum, 0.0)
    entropy = jnp.where(live, log_sum - moment / total, 0.0)
    logprob_ref[...] = logprob[0:req_dev, 0:pos_dev]
    entropy_ref[...] = entropy[0:req_dev, 0:pos_dev]

    part[0, :, :] = jnp.broadcast_to(jnp.sum(logprob, axis=1, keepdims=True), (8, LANES))
    for rel in range(1, 8):
        copy = pltpu.make_async_remote_copy(
            src_ref=part.at[0], dst_ref=part.at[rel],
            send_sem=part_send.at[rel], recv_sem=part_recv.at[rel],
            device_id=partner(rel), device_id_type=MESH_ID,
        )
        copy.start()
        started.append(copy)
    for rel in range(1, 8):
        pltpu.make_async_copy(part.at[rel], part.at[rel], part_recv.at[rel]).wait()
    pairs = [part[2 * i] + part[2 * i + 1] for i in range(4)]
    plane_sums[0, :, :] = (pairs[0] + pairs[1]) + (pairs[2] + pairs[3])
    for step in range(1, planes):
        copy = pltpu.make_async_remote_copy(
            src_ref=plane_sums.at[0], dst_ref=plane_sums.at[step],
            send_sem=plane_send.at[step], recv_sem=plane_recv.at[step],
            device_id=(lax.rem(plane + step, planes), me), device_id_type=MESH_ID,
        )
        copy.start()
        started.append(copy)
    for step in range(1, planes):
        pltpu.make_async_copy(plane_sums.at[step], plane_sums.at[step], plane_recv.at[step]).wait()

    count = planes * req_dev
    pieces = []
    for z in range(planes):
        chosen = plane_sums[0]
        for step in range(1, planes):
            chosen = jnp.where(lax.rem(z + step, planes) == plane, plane_sums[step], chosen)
        pieces.append(chosen[0:req_dev, :])
    column = jnp.concatenate(pieces, axis=0)
    row16 = lax.broadcasted_iota(jnp.int32, (count, LANES), 0)
    lane16 = lax.broadcasted_iota(jnp.int32, (count, LANES), 1)
    across = jnp.sum(jnp.where(row16 == lane16, column, 0.0), axis=0, keepdims=True)
    group_column = jnp.full((count, LANES), -1, jnp.int32)
    group_row = jnp.full((count, LANES), -2, jnp.int32)
    for j in range(count):
        group_column = jnp.where(row16 == j, groups_ref[j], group_column)
        group_row = jnp.where(lane16 == j, groups_ref[j], group_row)
    same = (group_column == group_row).astype(jnp.float32)
    members = jnp.sum(same, axis=0, keepdims=True)
    members = jnp.maximum(members, 1.0)
    mean = jnp.sum(same * column, axis=0, keepdims=True) / members
    spread = jnp.sum(same * (column - mean) ** 2, axis=0, keepdims=True) / members
    centered = (across - mean) / jnp.maximum(jnp.sqrt(spread), 1.0)
    centered_ref[...] = centered[:, 0:count]
    for copy in started:
        copy.wait_send()


def fused_body(planes, block, hidden, norm_gain, head_weight, token_ids, lengths, group_ids):
    req_dev, pos_dev, width = hidden.shape
    vocab_dev = head_weight.shape[1]
    padded = -(-vocab_dev // CHUNK) * CHUNK
    smem = pl.BlockSpec(memory_space=pltpu.SMEM)
    vmem = pl.BlockSpec(memory_space=pltpu.VMEM)
    dma = pltpu.SemaphoreType.DMA
    wide = pltpu.VMEM((block, LANES), jnp.float32)
    gathered = 8 * req_dev * pos_dev
    logprob, entropy, centered = pl.pallas_call(
        functools.partial(fused_kernel, planes),
        out_shape=(
            jax.ShapeDtypeStruct((req_dev, pos_dev), jnp.float32),
            jax.ShapeDtypeStruct((req_dev, pos_dev), jnp.float32),
            jax.ShapeDtypeStruct((1, planes * req_dev), jnp.float32),
        ),
        in_specs=[smem, smem, vmem, vmem, vmem, pl.BlockSpec(memory_space=pl.ANY)],
        out_specs=(vmem, vmem, vmem),
        scratch_shapes=[
            pltpu.VMEM((gathered, width), jnp.bfloat16),
            pltpu.VMEM((width, vocab_dev), jnp.bfloat16),
            pltpu.VMEM((block, padded), jnp.float32),
            pltpu.VMEM((block, padded), jnp.float32),
            wide, wide, wide, wide, wide,
            pltpu.VMEM((block, LANES), jnp.int32),
            pltpu.VMEM((8, 8, LANES), jnp.int32),
            pltpu.VMEM((8, 32, LANES), jnp.float32),
            pltpu.VMEM((8, 32, LANES), jnp.float32),
            pltpu.VMEM((8, 8, LANES), jnp.float32),
            pltpu.VMEM((planes, 8, LANES), jnp.float32),
            dma((8,)), dma((32,)), dma((32,)), dma((8,)), dma((8,)), dma((8,)), dma((8,)),
            dma((8,)), dma((8,)), dma((planes,)), dma((planes,)),
        ],
        compiler_params=pltpu.CompilerParams(
            collective_id=0, has_side_effects=True, vmem_limit_bytes=56 * 1024 * 1024
        ),
        cost_estimate=pl.CostEstimate(
            flops=2 * gathered * width * vocab_dev,
            bytes_accessed=2 * width * vocab_dev,
            transcendentals=gathered * vocab_dev,
        ),
        name="fused_scores",
    )(lengths, group_ids, hidden, norm_gain.reshape(1, width), token_ids, head_weight)
    return logprob, entropy, centered.reshape(planes * req_dev)


def slice_stats(rows, tokens, weight, offset):
    row_count = rows.shape[0]
    block_len = min(512, row_count)
    columns = jnp.arange(weight.shape[1], dtype=jnp.int32)
    results = []
    for block_start in range(0, row_count, block_len):
        block_rows = rows[block_start : block_start + block_len]
        local_ids = tokens[block_start : block_start + block_len] - offset
        logits = jnp.dot(block_rows, weight, preferred_element_type=jnp.float32)
        row_top = jnp.max(logits, axis=1)
        exps = jnp.exp(logits - row_top[:, None])
        exp_total = jnp.sum(exps, axis=1)
        moment = jnp.sum(exps * logits, axis=1)
        picked = jnp.sum(jnp.where(columns[None, :] == local_ids[:, None], logits, 0.0), axis=1)
        results.append((row_top, exp_total, moment, picked))
    return tuple((jnp.concatenate([item[slot] for item in results]) for slot in range(4)))


def body(hidden, norm_gain, head_weight, token_ids, lengths, group_ids):
    req_dev, pos_dev, model_width = hidden.shape
    vocab_dev = head_weight.shape[1]
    vocab_index = lax.axis_index("vocab")
    req_index = lax.axis_index("req")
    values = hidden.astype(jnp.float32)
    squares = jnp.mean(values * values, axis=-1, keepdims=True)
    normed = (values * lax.rsqrt(squares + norm_eps) * norm_gain).astype(jnp.bfloat16)
    own_rows = req_dev * pos_dev
    flat_rows = normed.reshape(own_rows, model_width)
    flat_tokens = token_ids.reshape(own_rows)
    offset = vocab_index * vocab_dev
    fresh = slice_stats(
        lax.all_gather(flat_rows, "vocab", axis=0, tiled=True),
        lax.all_gather(flat_tokens, "vocab", axis=0, tiled=True),
        head_weight,
        offset,
    )
    maxima, sums, moments, picked = tuple((new_part for new_part in fresh))
    own_start = vocab_index * own_rows
    row_top = lax.pmax(maxima, "vocab")
    rescale = jnp.exp(maxima - row_top)
    exp_total, moment, token_logit = lax.psum((sums * rescale, moments * rescale, picked), "vocab")
    row_top = lax.dynamic_slice_in_dim(row_top, own_start, own_rows)
    exp_total = lax.dynamic_slice_in_dim(exp_total, own_start, own_rows)
    moment = lax.dynamic_slice_in_dim(moment, own_start, own_rows)
    token_logit = lax.dynamic_slice_in_dim(token_logit, own_start, own_rows)
    log_total = row_top + jnp.log(exp_total)
    raw_logprob = (token_logit - log_total).reshape(req_dev, pos_dev)
    raw_entropy = (log_total - moment / exp_total).reshape(req_dev, pos_dev)
    positions = vocab_index * pos_dev + jnp.arange(pos_dev, dtype=jnp.int32)
    own_lengths = lax.dynamic_slice_in_dim(lengths, req_index * req_dev, req_dev)
    is_live = positions[None, :] < own_lengths[:, None]
    logprob = jnp.where(is_live, raw_logprob, 0.0)
    entropy = jnp.where(is_live, raw_entropy, 0.0)
    partial_sums = jnp.sum(logprob, axis=1)
    request_count = lengths.shape[0]
    global_rows = req_index * req_dev + jnp.arange(req_dev, dtype=jnp.int32)
    slots = jnp.arange(request_count, dtype=jnp.int32)
    placed = jnp.sum(
        jnp.where(slots[None, :] == global_rows[:, None], partial_sums[:, None], 0.0), axis=0
    )
    seq_sum = lax.psum(placed, ("req", "vocab"))
    same = (group_ids[:, None] == group_ids[None, :]).astype(jnp.float32)
    members = jnp.sum(same, axis=1)
    group_mean = jnp.sum(same * seq_sum[None, :], axis=1) / members
    spread = jnp.sum(same * (seq_sum[None, :] - group_mean[:, None]) ** 2, axis=1) / members
    group_std = jnp.maximum(jnp.sqrt(spread), 1.0)
    centered = (seq_sum - group_mean) / group_std
    return (logprob, entropy, centered)


def solution(mesh):
    plan = body
    if mesh.shape["vocab"] == 8:
        plan = functools.partial(fused_body, mesh.shape["req"], BLOCK)
    return jax.shard_map(
        plan,
        mesh=mesh,
        in_specs=(P("req", "vocab", None), P(), P(None, "vocab"), P("req", "vocab"), P(), P()),
        out_specs=(P("req", "vocab"), P("req", "vocab"), P()),
        check_vma=False,
    )
```
